32 devices in a mesh: seq: 32 (over z, y, x, core), dp: 1.
Axes of the slice: x: 2, y: 2, z: 4, core: 2. Of those that a mesh axis runs over, the one named last changes fastest.
Arguments:
- frames: bfloat16 [1, 4096, 1024], P('dp', 'seq'), may hold values from -36 to 36
- kernel: bfloat16 [31, 1024], replicated, may hold values from -1 to 1
- norm_gain: float32 [1024], replicated, may hold values from 0.5 to 1.5
- router: bfloat16 [1024, 8], replicated, may hold values from -0.1875 to 0.1875
- experts: int32 [1, 4096, 2], P('dp', 'seq'), may hold values from 0 to 7, all different within a row; in each aligned block of 128 rows (0 to 127, 128 to 255, ..., all dimensions but the last counted through in order) at most 64 rows name the same one
- w_in: bfloat16 [32, 1024, 512], P('seq'), may hold values from -0.1875 to 0.1875
- w_out: bfloat16 [32, 512, 1024], P('seq'), may hold values from -0.125 to 0.125
- cotangent: bfloat16 [1, 4096, 1024], P('dp', 'seq'), may hold values from -8 to 8
Outputs:
- mixed: bfloat16 [1, 4096, 1024], P('dp', 'seq')
- grad_frames: bfloat16 [1, 4096, 1024], P('dp', 'seq')
- grad_kernel: float32 [31, 1024], replicated
- grad_gain: float32 [1024], replicated
- grad_router: float32 [1024, 8], replicated
- grad_w_in: float32 [32, 1024, 512], P('seq')
- grad_w_out: float32 [32, 512, 1024], P('seq')
The draws below stay inside these ranges and needn't reach their ends.
Inputs may be any that keep to these rules, and one draw needn't show every extreme that they name: Each frame names 2 different experts; in each aligned block of 128 frames no expert is named more than 64 times, a bound that some block reaches.
All inputs are finite; a program needn't handle non-finite values.
Results may differ from the reference program's by a relative error of at most 0.0075.
Values may be sent and summed in bfloat16 or wider, within the bound.
A program may use at most 128 MiB of HBM per device.

```python
import math
import jax
import jax.numpy as jnp
import numpy as np
from jax import lax

D = 1024
FF = 2048
KW = 31
TOP = 2
GROUP = 4
TOK_DEV = 128
EXPERTS = 8
HID_DEV = 512
CAP = 64
FRAMES = 4096
RECS = 1
N_SEQ = 32


def draw_frames(key, part):
    first_key, row_key, col_key = jax.random.split(key, 3)
    values = jnp.clip(jax.random.normal(first_key, (RECS, FRAMES, D), jnp.float32), -4.0, 4.0)
    row_scale = jnp.exp(jax.random.uniform(row_key, (RECS, FRAMES, 1), jnp.float32, math.log(0.3), math.log(3.0)))
    col_scale = jnp.exp(jax.random.uniform(col_key, (1, 1, D), jnp.float32, math.log(0.3), math.log(3.0)))
    return (values * row_scale * col_scale).astype(jnp.bfloat16)


def draw_cotangent(key, part):
    first_key = jax.random.fold_in(key, 0)
    values = jnp.clip(jax.random.normal(first_key, (RECS, FRAMES, D), jnp.float32), -4.0, 4.0)
    ramp = 0.5 + 1.5 * jnp.arange(FRAMES, dtype=jnp.float32) / FRAMES
    return (values * ramp[None, :, None]).astype(jnp.bfloat16)


def shard_levels(rng, extent, pieces, least, largest):
    def one(axis_at, parts):
        draws = jax.random.uniform(jax.random.fold_in(jax.random.fold_in(rng, 6), axis_at), (parts,), jnp.float32, least / len(pieces), largest / len(pieces))
        return jnp.repeat(jnp.exp(draws), extent[axis_at] // parts).reshape((-1,) + (1,) * (len(extent) - axis_at - 1))

    loudness = one(*pieces[0])
    for cut in pieces[1:]:
        loudness = loudness * one(*cut)
    return loudness


def routed_block(key, own, number, rows, amount, top, most, lean):
    order = jax.random.permutation(key, amount)
    heavy_load, ordinary = load_shares(amount, rows * top, most, lean, True), load_shares(amount, rows * top, most, lean, False)
    places = jnp.arange(amount)

    def named(sizes, turn):
        used = int((sizes > 0).sum())
        fixed = max(1, used // 4)
        passed = fixed + (places - fixed + turn * (used - fixed)) % max(1, amount - fixed)
        return jnp.zeros((amount,), jnp.int32).at[order[jnp.where(places < fixed, places, passed)]].set(jnp.asarray(sizes, jnp.int32))

    sizes = jnp.where(number % 4 == 0, named(heavy_load, number // 4), named(ordinary, number - number // 4 - 1))
    mixed = jax.random.permutation(jax.random.fold_in(own, 3), amount)
    donor, sink = mixed[0:amount // 2 * 2:2], mixed[1:amount // 2 * 2:2]
    slack = jnp.minimum(sizes[donor] - 1, most - sizes[sink]) // 2
    slack = jnp.where((donor == order[0]) | (sink == order[0]) | (sizes[sink] == 0), 0, jnp.maximum(slack, 0))
    passed = jax.random.randint(jax.random.fold_in(own, 4), (amount // 2,), 0, 1 << 20) % (slack + 1)
    sizes = sizes.at[donor].add(-passed).at[sink].add(passed)
    members = jnp.searchsorted(jnp.cumsum(sizes), jnp.arange(rows * top), side="right").astype(jnp.int32)
    grid = members.reshape(top, rows).T
    grid = grid[jax.random.permutation(jax.random.fold_in(own, 1), rows)]
    turn = jax.random.randint(jax.random.fold_in(own, 2), (rows, 1), 0, top)
    return jnp.take_along_axis(grid, (jnp.arange(top)[None, :] + turn) % top, axis=1)


def load_shares(amount, total, limit, skew, full):
    portions = [(1 << 20) // math.isqrt(grade ** skew) + 1 for grade in range(1, amount + 1)]
    largest = limit if full else min(limit, max(-(-total // amount), total * portions[0] // sum(portions)))
    least = 1 if total - largest >= amount - 1 else 0
    counts, spare = [largest] + [least] * (amount - 1), total - largest - least * (amount - 1)
    while spare > 0:
        free = [i for i in range(1, amount) if counts[i] < largest] or [i for i in range(1, amount) if counts[i] < limit]
        pool, left = sum([portions[i] for i in free]), spare
        for i in free:
            extra = min(limit - counts[i], max(1, left * portions[i] // pool), spare)
            counts[i] = counts[i] + extra
            spare = spare - extra
    return np.array(counts)


def gaussian(own_key, shape, spread, most, cuts=(), kind=jnp.bfloat16):
    drawn = spread * jax.random.normal(own_key, shape, jnp.float32)
    if cuts:
        drawn = drawn * shard_levels(own_key, shape, cuts, -0.22, 0.18)
    return jnp.clip(drawn, -most, most).astype(kind)


def setup_inputs(seed: int = 0) -> dict:
    streams_of = jax.random.split(jax.random.key(seed), 9)
    frames = draw_frames(jax.random.fold_in(streams_of[8], 71), 0)
    kernel = gaussian(streams_of[1], (KW, D), KW ** -0.5, 1.0)
    norm_gain = jnp.clip(1.0 + 0.1 * jax.random.normal(streams_of[2], (D,), jnp.float32), 0.5, 1.5)
    router = gaussian(streams_of[3], (D, EXPERTS), D ** -0.5, 0.1875)
    experts_keys = jax.random.split(jax.random.fold_in(streams_of[4], 1), RECS * FRAMES // TOK_DEV)
    experts_turns = jax.random.permutation(jax.random.fold_in(streams_of[4], 3), RECS * FRAMES // TOK_DEV)
    experts = jax.vmap(lambda own, number: routed_block(jax.random.fold_in(streams_of[4], 2), own, number, TOK_DEV, EXPERTS, TOP, CAP, 2))(experts_keys, experts_turns).reshape((RECS, FRAMES, TOP))
    w_in = gaussian(streams_of[5], (N_SEQ, D, HID_DEV), D ** -0.5, 0.1875, ((0, 32),))
    w_out = gaussian(streams_of[6], (N_SEQ, HID_DEV, D), FF ** -0.5, 0.125, ((0, 32),))
    cotangent = draw_cotangent(jax.random.fold_in(streams_of[8], 71), 0)
    return dict(frames=frames, kernel=kernel, norm_gain=norm_gain, router=router, experts=experts, w_in=w_in, w_out=w_out, cotangent=cotangent)


eps = 1e-06

def conv_forward(padded, kernel, row_count):
    summed = jnp.zeros((row_count, padded.shape[1]), jnp.float32)
    for offset in range(kernel.shape[0]):
        summed = summed + kernel[offset].astype(jnp.float32) * padded[offset:offset + row_count].astype(jnp.float32)
    return summed

def conv_transpose(padded, kernel, row_count):
    length = kernel.shape[0]
    summed = jnp.zeros((row_count, padded.shape[1]), jnp.float32)
    for offset in range(length):
        start = length - 1 - offset
        summed = summed + kernel[offset].astype(jnp.float32) * padded[start:start + row_count]
    return summed

def kernel_terms(padded, upstream, length, row_count):
    return jnp.stack([lax.optimization_barrier(jnp.sum(padded[offset:offset + row_count].astype(jnp.float32) * upstream, axis=0)) for offset in range(length)])

def normalize(summed, norm_gain):
    square = lax.optimization_barrier(jnp.mean(summed * summed, axis=-1, keepdims=True))
    return summed * lax.rsqrt(square + eps) * norm_gain

def slot_numbers(expert_ids, expert_count):
    onehot = (expert_ids[:, None] == jnp.arange(expert_count, dtype=jnp.int32)[None, :]).astype(jnp.int32)
    ranks = jnp.cumsum(onehot, axis=0) - onehot
    return lax.optimization_barrier(jnp.sum(ranks * onehot, axis=1)).astype(jnp.int32)

def gate_values(normed_b, router, first_ids, second_ids):
    logits = jnp.dot(normed_b, router, preferred_element_type=jnp.float32)
    columns = jnp.arange(router.shape[1], dtype=jnp.int32)[None, :]
    pick_diff = (first_ids[:, None] == columns).astype(jnp.float32) - (second_ids[:, None] == columns).astype(jnp.float32)
    gate_one = jax.nn.sigmoid(lax.optimization_barrier(jnp.sum(logits * pick_diff, axis=1)))
    return (gate_one, 1.0 - gate_one, pick_diff)

def swish_parts(pre_act):
    squash = jax.nn.sigmoid(pre_act)
    return (pre_act * squash, squash * (1.0 + pre_act * (1.0 - squash)))

def gate_backward(upstream, out_one, out_two, gate_one, gate_two, pick_diff, normed_b, router):
    grad_gap = (lax.optimization_barrier(jnp.sum(upstream * out_one, axis=1)) - lax.optimization_barrier(jnp.sum(upstream * out_two, axis=1))) * gate_one * gate_two
    grad_logits = (grad_gap[:, None] * pick_diff).astype(jnp.bfloat16)
    router_term = jnp.dot(normed_b.T, grad_logits, preferred_element_type=jnp.float32)
    normed_term = jnp.dot(grad_logits, router.T, preferred_element_type=jnp.float32)
    return (router_term, normed_term)

def reference(frames, kernel, norm_gain, router, experts, w_in, w_out, cotangent):
    half_width = KW // 2
    group_rows = N_SEQ * CAP
    assign_count = FRAMES * TOP
    outputs = []
    frame_grads = []
    grad_kernel = jnp.zeros((KW, D), jnp.float32)
    grad_gain = jnp.zeros((D,), jnp.float32)
    grad_router = jnp.zeros((D, EXPERTS), jnp.float32)
    grad_in = jnp.zeros((N_SEQ, D, HID_DEV), jnp.float32)
    grad_out = jnp.zeros((N_SEQ, HID_DEV, D), jnp.float32)
    for recording in range(RECS):
        inputs_rec = frames[recording]
        padded = jnp.pad(inputs_rec, ((half_width, half_width), (0, 0)))
        summed = inputs_rec.astype(jnp.float32) + conv_forward(padded, kernel, FRAMES)
        normed_b = normalize(summed, norm_gain).astype(jnp.bfloat16)
        choice_ids = experts[recording]
        gate_one, gate_two, pick_diff = gate_values(normed_b, router, choice_ids[:, 0], choice_ids[:, 1])
        block_ids = choice_ids.reshape(N_SEQ, TOK_DEV * TOP)
        block_slots = jax.vmap(lambda values: slot_numbers(values, EXPERTS))(block_ids)
        sources = jnp.arange(N_SEQ, dtype=jnp.int32)[:, None]
        position = (sources * CAP + block_slots).reshape(-1).astype(jnp.int32)
        flat_ids = block_ids.reshape(-1)
        lookup = jnp.full((EXPERTS, group_rows), assign_count, jnp.int32)
        lookup = lookup.at[flat_ids, position].set(jnp.arange(assign_count, dtype=jnp.int32))
        gather_index = (flat_ids * group_rows + position).astype(jnp.int32)
        spread_rows = jnp.concatenate([jnp.repeat(normed_b, TOP, axis=0), jnp.zeros((1, D), jnp.bfloat16)], axis=0)

        def expert_forward(expert):
            arrived = jnp.take(spread_rows, lookup[expert], axis=0)
            in_block = lax.dynamic_slice_in_dim(w_in, (expert * GROUP).astype(jnp.int32), GROUP, 0)
            out_block = lax.dynamic_slice_in_dim(w_out, (expert * GROUP).astype(jnp.int32), GROUP, 0)
            combined = jnp.zeros((group_rows, D), jnp.float32)
            for member in range(GROUP):
                pre_act = jnp.dot(arrived, in_block[member], preferred_element_type=jnp.float32)
                hidden = swish_parts(pre_act)[0].astype(jnp.bfloat16)
                partial_out = jnp.dot(hidden, out_block[member], preferred_element_type=jnp.float32)
                combined = combined + lax.optimization_barrier(partial_out.astype(jnp.bfloat16)).astype(jnp.float32)
            return combined
        expert_out = lax.map(expert_forward, jnp.arange(EXPERTS, dtype=jnp.int32)).reshape(EXPERTS * group_rows, D)
        assigned = jnp.take(expert_out, gather_index, axis=0).reshape(FRAMES, TOP, D)
        out_one = assigned[:, 0]
        out_two = assigned[:, 1]
        outputs.append((summed + gate_one[:, None] * out_one + gate_two[:, None] * out_two).astype(jnp.bfloat16))
        upstream = cotangent[recording].astype(jnp.float32)
        grad_assigned = jnp.stack([gate_one[:, None] * upstream, gate_two[:, None] * upstream], axis=1)
        grad_assigned = grad_assigned.reshape(assign_count, D).astype(jnp.bfloat16)
        spread_grads = jnp.concatenate([grad_assigned, jnp.zeros((1, D), jnp.bfloat16)], axis=0)

        def expert_backward(expert):
            arrived = jnp.take(spread_rows, lookup[expert], axis=0)
            incoming = jnp.take(spread_grads, lookup[expert], axis=0)
            in_block = lax.dynamic_slice_in_dim(w_in, (expert * GROUP).astype(jnp.int32), GROUP, 0)
            out_block = lax.dynamic_slice_in_dim(w_out, (expert * GROUP).astype(jnp.int32), GROUP, 0)
            grad_rows = jnp.zeros((group_rows, D), jnp.float32)
            in_terms = []
            out_terms = []
            for member in range(GROUP):
                pre_act = jnp.dot(arrived, in_block[member], preferred_element_type=jnp.float32)
                hidden_f, slope = swish_parts(pre_act)
                hidden = hidden_f.astype(jnp.bfloat16)
                grad_hidden = jnp.dot(incoming, out_block[member].T, preferred_element_type=jnp.float32)
                grad_pre = (grad_hidden * slope).astype(jnp.bfloat16)
                out_terms.append(jnp.dot(hidden.T, incoming, preferred_element_type=jnp.float32))
                in_terms.append(jnp.dot(arrived.T, grad_pre, preferred_element_type=jnp.float32))
                grad_part = jnp.dot(grad_pre, in_block[member].T, preferred_element_type=jnp.float32)
                grad_rows = grad_rows + lax.optimization_barrier(grad_part.astype(jnp.bfloat16)).astype(jnp.float32)
            return (grad_rows, jnp.stack(in_terms), jnp.stack(out_terms))
        grad_rows, in_terms, out_terms = lax.map(expert_backward, jnp.arange(EXPERTS, dtype=jnp.int32))
        grad_in = grad_in + in_terms.reshape(N_SEQ, D, HID_DEV)
        grad_out = grad_out + out_terms.reshape(N_SEQ, HID_DEV, D)
        normed_grads = jnp.take(grad_rows.reshape(EXPERTS * group_rows, D), gather_index, axis=0)
        normed_grads = lax.optimization_barrier(jnp.sum(normed_grads.reshape(FRAMES, TOP, D), axis=1))
        router_term, normed_term = gate_backward(upstream, out_one, out_two, gate_one, gate_two, pick_diff, normed_b, router)
        pullback = jax.vjp(normalize, summed, norm_gain)[1]
        summed_grad, gain_term = pullback(normed_grads + normed_term)
        upstream_total = upstream + summed_grad
        padded_grad = jnp.pad(upstream_total, ((half_width, half_width), (0, 0)))
        frame_grads.append((upstream_total + conv_transpose(padded_grad, kernel, FRAMES)).astype(jnp.bfloat16))
        grad_kernel = grad_kernel + kernel_terms(padded, upstream_total, KW, FRAMES)
        grad_gain = grad_gain + gain_term
        grad_router = grad_router + router_term
    return (jnp.stack(outputs), jnp.stack(frame_grads), grad_kernel, grad_gain, grad_router, grad_in, grad_out)
```

```python
import jax
import jax.numpy as jnp
from jax import lax
from jax.experimental import pallas as pl
from jax.experimental.pallas import tpu as pltpu
from jax.sharding import PartitionSpec as P

MESH = pl.DeviceIdType.MESH

eps = 1e-06


def padded_2(shard, sides, width):
    for axis, dim in sides:
        size, length = (lax.axis_size(axis), shard.shape[dim])
        up = [(i, (i + 1) % size) for i in range(size - 1)]
        down = [(j, i) for i, j in up]
        last = lax.slice_in_dim(shard, length - width, length, axis=dim)
        initial = lax.slice_in_dim(shard, 0, width, axis=dim)
        before = lax.ppermute(last, axis, up)
        after = lax.ppermute(initial, axis, down)
        shard = jnp.concatenate([before, shard, after], axis=dim)
    return shard


def conv_forward(padded, kernel, row_count):
    summed = jnp.zeros((row_count, padded.shape[1]), jnp.float32)
    for offset in range(kernel.shape[0]):
        summed = summed + kernel[offset].astype(jnp.float32) * padded[
            offset : offset + row_count
        ].astype(jnp.float32)
    return summed


def conv_transpose(padded, kernel, row_count):
    length = kernel.shape[0]
    summed = jnp.zeros((row_count, padded.shape[1]), jnp.float32)
    for offset in range(length):
        start = length - 1 - offset
        summed = summed + kernel[offset].astype(jnp.float32) * padded[start : start + row_count]
    return summed


def kernel_terms(padded, upstream, length, row_count):
    return jnp.stack(
        [
            jnp.sum(padded[offset : offset + row_count].astype(jnp.float32) * upstream, axis=0)
            for offset in range(length)
        ]
    )


def normalize(summed, norm_gain):
    square = jnp.mean(summed * summed, axis=-1, keepdims=True)
    return summed * lax.rsqrt(square + eps) * norm_gain


def slot_numbers(expert_ids, expert_count):
    onehot = (expert_ids[:, None] == jnp.arange(expert_count, dtype=jnp.int32)[None, :]).astype(
        jnp.int32
    )
    ranks = jnp.cumsum(onehot, axis=0) - onehot
    return jnp.sum(ranks * onehot, axis=1)


def gate_values(normed_b, router, first_ids, second_ids):
    logits = jnp.dot(normed_b, router, preferred_element_type=jnp.float32)
    columns = jnp.arange(router.shape[1], dtype=jnp.int32)[None, :]
    pick_diff = (first_ids[:, None] == columns).astype(jnp.float32) - (
        second_ids[:, None] == columns
    ).astype(jnp.float32)
    gate_one = jax.nn.sigmoid(jnp.sum(logits * pick_diff, axis=1))
    return (gate_one, 1.0 - gate_one, pick_diff)


def swish_parts(pre_act):
    squash = jax.nn.sigmoid(pre_act)
    return (pre_act * squash, squash * (1.0 + pre_act * (1.0 - squash)))


def gate_backward(upstream, out_one, out_two, gate_one, gate_two, pick_diff, normed_b, router):
    grad_gap = (
        (jnp.sum(upstream * out_one, axis=1) - jnp.sum(upstream * out_two, axis=1))
        * gate_one
        * gate_two
    )
    grad_logits = (grad_gap[:, None] * pick_diff).astype(jnp.bfloat16)
    router_term = jnp.dot(normed_b.T, grad_logits, preferred_element_type=jnp.float32)
    normed_term = jnp.dot(grad_logits, router.T, preferred_element_type=jnp.float32)
    return (router_term, normed_term)


def dot_over(left, right, left_dim, right_dim):
    return lax.dot_general(
        left, right, (((left_dim,), (right_dim,)), ((), ())), preferred_element_type=jnp.float32
    )


def moe_kernel(
    packed, w_in, w_out, back, grad_in, grad_out,
    rows, part, core_got, x_send, x_got, kept, final, sems,
):
    count, cap, width = packed.shape
    depth = width // 2
    me = lax.axis_index("seq")
    e, x, c = me // 4, (me % 4) // 2, me % 2
    own = c * 2 + x
    own_x = c * 2 + 1 - x
    other = (1 - c) * 2 + x
    other_x = (1 - c) * 2 + 1 - x

    def place(e_to, x_to, c_to):
        return {"seq": e_to * 4 + x_to * 2 + c_to}

    core_peer, x_peer = place(e, x, 1 - c), place(e, 1 - x, c)

    def copy(kind, k, source, target, device):
        return pltpu.make_async_remote_copy(
            src_ref=source,
            dst_ref=target,
            send_sem=sems.at[0, kind, k],
            recv_sem=sems.at[1, kind, k],
            device_id=device,
            device_id_type=MESH,
        )

    def block(k):
        return (e + count - k) % count

    def dispatch(k):
        to = (e + k) % count
        return copy(0, k, packed.at[to], rows.at[e, own], place(to, x, c))

    def near(kind, k, section, device):
        piece = rows.at[block(k), section]
        return copy(kind, k, piece, piece, device)

    def core_sum(k):
        f = block(k)
        return copy(4, k, part.at[f, pl.ds((1 - c) * 2, 2)], core_got.at[f], core_peer)

    def x_sum(k):
        f = block(k)
        return copy(5, k, x_send.at[f], x_got.at[f], x_peer)

    def give_back(k, slot):
        f = block(k)
        return copy(6, k, final.at[f], back.at[slot], place(f, x, c))

    barrier = pltpu.get_barrier_semaphore()
    pl.semaphore_signal(barrier, inc=1, device_id=core_peer, device_id_type=MESH)
    pl.semaphore_signal(barrier, inc=1, device_id=x_peer, device_id_type=MESH)

    def greet(k, carry):
        pl.semaphore_signal(
            barrier, inc=1, device_id=place((e + k) % count, x, c), device_id_type=MESH
        )
        return carry

    lax.fori_loop(1, count, greet, 0)
    pl.semaphore_wait(barrier, count + 1)

    def send_first(k, carry):
        dispatch(k).start()
        return carry

    lax.fori_loop(1, count, send_first, 0)
    rows[e, own] = packed[e]
    grad_in[...] = jnp.zeros_like(grad_in)
    grad_out[...] = jnp.zeros_like(grad_out)

    def stage_spread(k):
        f = block(k)

        @pl.when(k > 0)
        def _():
            copy(0, k, packed.at[f], rows.at[f, own], place(f, x, c)).wait_recv()

        near(1, k, own, x_peer).start()
        near(2, k, own, core_peer).start()

    def stage_forward(k):
        near(1, k, own_x, x_peer).wait_recv()
        near(3, k, own_x, core_peer).start()

    def stage_compute(k):
        f = block(k)
        near(2, k, other, core_peer).wait_recv()
        near(3, k, other_x, core_peer).wait_recv()
        values = rows[f].reshape(4 * cap, width)
        normed, grads = values[:, :depth], values[:, depth:]
        pre_act = dot_over(normed, w_in[...], 1, 0)
        hidden_f, slope = swish_parts(pre_act)
        hidden = hidden_f.astype(jnp.bfloat16)
        grad_pre = (dot_over(grads, w_out[...], 1, 1) * slope).astype(jnp.bfloat16)
        part[f, :, :, :depth] = (
            dot_over(hidden, w_out[...], 1, 0).astype(jnp.bfloat16).reshape(4, cap, depth)
        )
        part[f, :, :, depth:] = (
            dot_over(grad_pre, w_in[...], 1, 1).astype(jnp.bfloat16).reshape(4, cap, depth)
        )
        core_sum(k).start()
        grad_out[...] += dot_over(hidden, grads, 0, 0)
        grad_in[...] += dot_over(normed, grad_pre, 0, 0)

    def stage_core(k):
        f = block(k)
        core_sum(k).wait_recv()
        x_send[f] = (
            part[f, own_x].astype(jnp.float32) + core_got[f, 1 - x].astype(jnp.float32)
        ).astype(jnp.bfloat16)
        x_sum(k).start()
        kept[f] = part[f, own].astype(jnp.float32) + core_got[f, x].astype(jnp.float32)

    def stage_back(k):
        f = block(k)
        x_sum(k).wait_recv()
        total = (kept[f] + x_got[f].astype(jnp.float32)).astype(jnp.bfloat16)

        @pl.when(k == 0)
        def _():
            back[e] = total

        @pl.when(k > 0)
        def _():
            final[f] = total
            give_back(k, e).start()

    stages = (stage_back, stage_core, stage_compute, stage_forward, stage_spread)

    def step(t, carry):
        for lag, stage in zip((4, 3, 2, 1, 0), stages):
            k = t - lag

            @pl.when((k >= 0) & (k < count))
            def _(stage=stage, k=k):
                stage(k)

        return carry

    lax.fori_loop(0, count + 4, step, 0)

    def finish(k, carry):
        @pl.when(k > 0)
        def _():
            dispatch(k).wait_send()
            give_back(k, e).wait_send()
            give_back(k, (e + k) % count).wait_recv()

        near(1, k, own, x_peer).wait_send()
        near(2, k, own, core_peer).wait_send()
        near(3, k, own_x, core_peer).wait_send()
        core_sum(k).wait_send()
        x_sum(k).wait_send()
        return carry

    lax.fori_loop(0, count, finish, 0)


def moe(packed, w_in, w_out):
    count, cap, width = packed.shape
    vmem = pl.BlockSpec(memory_space=pltpu.VMEM)
    half = jnp.bfloat16
    return pl.pallas_call(
        moe_kernel,
        out_shape=(
            jax.ShapeDtypeStruct(packed.shape, half),
            jax.ShapeDtypeStruct(w_in.shape, jnp.float32),
            jax.ShapeDtypeStruct(w_out.shape, jnp.float32),
        ),
        in_specs=[vmem] * 3,
        out_specs=(vmem,) * 3,
        scratch_shapes=[
            pltpu.VMEM((count, 4, cap, width), half),
            pltpu.VMEM((count, 4, cap, width), half),
            pltpu.VMEM((count, 2, cap, width), half),
            pltpu.VMEM((count, cap, width), half),
            pltpu.VMEM((count, cap, width), half),
            pltpu.VMEM((count, cap, width), jnp.float32),
            pltpu.VMEM((count, cap, width), half),
            pltpu.SemaphoreType.DMA((2, 7, count)),
        ],
        compiler_params=pltpu.CompilerParams(
            collective_id=0, has_side_effects=True, vmem_limit_bytes=56 * 2**20
        ),
    )(packed, w_in, w_out)


def sum_kernel(terms, totals, got, sems):
    count = terms.shape[0]
    seq_size = lax.axis_size("seq")
    me = lax.axis_index("dp") * seq_size + lax.axis_index("seq")

    def place(number):
        return {"dp": number // seq_size, "seq": number % seq_size}

    def copy(phase, j, source, target, number):
        return pltpu.make_async_remote_copy(
            src_ref=source,
            dst_ref=target,
            send_sem=sems.at[phase, 0, j],
            recv_sem=sems.at[phase, 1, j],
            device_id=place(number),
            device_id_type=MESH,
        )

    def ahead(j):
        return (me + j) % count

    def behind(j):
        return (me + count - j) % count

    def every(action):
        def one(j, carry):
            action(j)
            return carry

        lax.fori_loop(1, count, one, 0)

    barrier = pltpu.get_barrier_semaphore()
    every(
        lambda j: pl.semaphore_signal(
            barrier, inc=1, device_id=place(ahead(j)), device_id_type=MESH
        )
    )
    pl.semaphore_wait(barrier, count - 1)
    every(lambda j: copy(0, j, terms.at[ahead(j)], got.at[me], ahead(j)).start())
    got[me] = terms[me]
    every(lambda j: copy(0, j, terms.at[ahead(j)], got.at[behind(j)], ahead(j)).wait_recv())
    totals[me] = jnp.sum(got[...], axis=0)
    every(lambda j: copy(1, j, totals.at[me], totals.at[me], ahead(j)).start())
    every(lambda j: copy(1, j, totals.at[me], totals.at[behind(j)], ahead(j)).wait_recv())
    every(lambda j: copy(0, j, terms.at[ahead(j)], got.at[me], ahead(j)).wait_send())
    every(lambda j: copy(1, j, totals.at[me], totals.at[me], ahead(j)).wait_send())


def sum_everywhere(values):
    count = lax.axis_size("seq") * lax.axis_size("dp")
    flat = jnp.concatenate([value.reshape(-1) for value in values])
    tall = -(-flat.shape[0] // (count * 1024)) * 8
    padded = jnp.pad(flat, (0, count * tall * 128 - flat.shape[0])).reshape(count, tall, 128)
    vmem = pl.BlockSpec(memory_space=pltpu.VMEM)
    totals = pl.pallas_call(
        sum_kernel,
        out_shape=jax.ShapeDtypeStruct(padded.shape, jnp.float32),
        in_specs=[vmem],
        out_specs=vmem,
        scratch_shapes=[
            pltpu.VMEM(padded.shape, jnp.float32),
            pltpu.SemaphoreType.DMA((2, 2, count)),
        ],
        compiler_params=pltpu.CompilerParams(collective_id=1, has_side_effects=True),
    )(padded).reshape(-1)
    results, start = [], 0
    for value in values:
        results.append(totals[start : start + value.size].reshape(value.shape))
        start += value.size
    return results


def body(frames, kernel, norm_gain, router, experts, w_in, w_out, cotangent):
    inputs_dev = frames[0]
    row_count = inputs_dev.shape[0]
    width = inputs_dev.shape[1]
    length = kernel.shape[0]
    half_width = length // 2
    expert_count = router.shape[1]
    top_count = experts.shape[2]
    capacity = 2 * row_count * top_count // expert_count
    in_weights = w_in[0]
    out_weights = w_out[0]
    padded = padded_2(inputs_dev, (("seq", 0),), half_width)
    summed = inputs_dev.astype(jnp.float32) + conv_forward(padded, kernel, row_count)
    normed_b = normalize(summed, norm_gain).astype(jnp.bfloat16)
    choice_ids = experts[0]
    gate_one, gate_two, pick_diff = gate_values(
        normed_b, router, choice_ids[:, 0], choice_ids[:, 1]
    )
    flat_ids = choice_ids.reshape(-1)
    slot_index = slot_numbers(flat_ids, expert_count)
    position = flat_ids * capacity + slot_index
    dispatch_table = (
        lax.broadcasted_iota(jnp.int32, (expert_count * capacity, flat_ids.shape[0]), 0)
        == position[None, :]
    ).astype(jnp.bfloat16)

    def pack(values):
        return jnp.dot(dispatch_table, values, preferred_element_type=jnp.float32).astype(
            jnp.bfloat16
        )

    repeated = jnp.repeat(normed_b, top_count, axis=0)
    upstream = cotangent[0].astype(jnp.float32)
    grad_assigned = jnp.stack([gate_one[:, None] * upstream, gate_two[:, None] * upstream], axis=1)
    grad_values = grad_assigned.reshape(row_count * top_count, width).astype(jnp.bfloat16)
    packed = pack(jnp.concatenate([repeated, grad_values], axis=1))
    back, in_term, out_term = moe(
        packed.reshape(expert_count, capacity, 2 * width), in_weights, out_weights
    )
    back = back.reshape(expert_count * capacity, 2 * width)
    assigned = dot_over(dispatch_table, back[:, :width], 0, 0).reshape(
        row_count, top_count, width
    )
    out_one = assigned[:, 0]
    out_two = assigned[:, 1]
    mixed = (summed + gate_one[:, None] * out_one + gate_two[:, None] * out_two).astype(
        jnp.bfloat16
    )
    both = jnp.sum(dispatch_table.reshape(-1, row_count, top_count), axis=2)
    normed_grads = dot_over(both, back[:, width:], 0, 0)
    router_term, normed_term = gate_backward(
        upstream, out_one, out_two, gate_one, gate_two, pick_diff, normed_b, router
    )
    pullback = jax.vjp(normalize, summed, norm_gain)[1]
    summed_grad, gain_term = pullback(normed_grads + normed_term)
    upstream_total = upstream + summed_grad
    padded_grad = padded_2(upstream_total.astype(jnp.bfloat16), (("seq", 0),), half_width).astype(
        upstream_total.dtype
    )
    grad_frames = (upstream_total + conv_transpose(padded_grad, kernel, row_count)).astype(
        jnp.bfloat16
    )
    kernel_term = kernel_terms(padded, upstream_total, length, row_count)
    grad_kernel, grad_gain, grad_router = sum_everywhere((kernel_term, gain_term, router_term))
    grad_in, grad_out = in_term, out_term
    if lax.axis_size("dp") > 1:
        grad_in, grad_out = (
            lax.psum(in_term.astype(jnp.bfloat16), "dp").astype(jnp.float32),
            lax.psum(out_term.astype(jnp.bfloat16), "dp").astype(jnp.float32),
        )
    return (
        mixed[None],
        grad_frames[None],
        grad_kernel,
        grad_gain,
        grad_router,
        grad_in[None],
        grad_out[None],
    )


def solution(mesh):
    return jax.shard_map(
        body,
        mesh=mesh,
        in_specs=(
            P("dp", "seq", None),
            P(),
            P(),
            P(),
            P("dp", "seq", None),
            P("seq", None, None),
            P("seq", None, None),
            P("dp", "seq", None),
        ),
        out_specs=(
            P("dp", "seq", None),
            P("dp", "seq", None),
            P(),
            P(),
            P(),
            P("seq", None, None),
            P("seq", None, None),
        ),
        check_vma=False,
    )
```

```python
import jax
import jax.numpy as jnp
from jax import lax
from jax.experimental import pallas as pl
from jax.experimental.pallas import tpu as pltpu
from jax.sharding import PartitionSpec as P

MESH = pl.DeviceIdType.MESH

eps = 1e-06


def padded_2(shard, sides, width):
    for axis, dim in sides:
        size, length = (lax.axis_size(axis), shard.shape[dim])
        up = [(i, (i + 1) % size) for i in range(size - 1)]
        down = [(j, i) for i, j in up]
        last = lax.slice_in_dim(shard, length - width, length, axis=dim)
        initial = lax.slice_in_dim(shard, 0, width, axis=dim)
        before = lax.ppermute(last, axis, up)
        after = lax.ppermute(initial, axis, down)
        shard = jnp.concatenate([before, shard, after], axis=dim)
    return shard


def conv_forward(padded, kernel, row_count):
    summed = jnp.zeros((row_count, padded.shape[1]), jnp.float32)
    for offset in range(kernel.shape[0]):
        summed = summed + kernel[offset].astype(jnp.float32) * padded[
            offset : offset + row_count
        ].astype(jnp.float32)
    return summed


def conv_transpose(padded, kernel, row_count):
    length = kernel.shape[0]
    summed = jnp.zeros((row_count, padded.shape[1]), jnp.float32)
    for offset in range(length):
        start = length - 1 - offset
        summed = summed + kernel[offset].astype(jnp.float32) * padded[start : start + row_count]
    return summed


def kernel_terms(padded, upstream, length, row_count):
    return jnp.stack(
        [
            jnp.sum(padded[offset : offset + row_count].astype(jnp.float32) * upstream, axis=0)
            for offset in range(length)
        ]
    )


def normalize(summed, norm_gain):
    square = jnp.mean(summed * summed, axis=-1, keepdims=True)
    return summed * lax.rsqrt(square + eps) * norm_gain


def slot_numbers(expert_ids, expert_count):
    onehot = (expert_ids[:, None] == jnp.arange(expert_count, dtype=jnp.int32)[None, :]).astype(
        jnp.int32
    )
    ranks = jnp.cumsum(onehot, axis=0) - onehot
    return jnp.sum(ranks * onehot, axis=1)


def gate_values(normed_b, router, first_ids, second_ids):
    logits = jnp.dot(normed_b, router, preferred_element_type=jnp.float32)
    columns = jnp.arange(router.shape[1], dtype=jnp.int32)[None, :]
    pick_diff = (first_ids[:, None] == columns).astype(jnp.float32) - (
        second_ids[:, None] == columns
    ).astype(jnp.float32)
    gate_one = jax.nn.sigmoid(jnp.sum(logits * pick_diff, axis=1))
    return (gate_one, 1.0 - gate_one, pick_diff)


def swish_parts(pre_act):
    squash = jax.nn.sigmoid(pre_act)
    return (pre_act * squash, squash * (1.0 + pre_act * (1.0 - squash)))


def gate_backward(upstream, out_one, out_two, gate_one, gate_two, pick_diff, normed_b, router):
    grad_gap = (
        (jnp.sum(upstream * out_one, axis=1) - jnp.sum(upstream * out_two, axis=1))
        * gate_one
        * gate_two
    )
    grad_logits = (grad_gap[:, None] * pick_diff).astype(jnp.bfloat16)
    router_term = jnp.dot(normed_b.T, grad_logits, preferred_element_type=jnp.float32)
    normed_term = jnp.dot(grad_logits, router.T, preferred_element_type=jnp.float32)
    return (router_term, normed_term)


def dot_over(left, right, left_dim, right_dim):
    return lax.dot_general(
        left, right, (((left_dim,), (right_dim,)), ((), ())), preferred_element_type=jnp.float32
    )


def moe_kernel(
    packed, w_in, w_out, back, grad_in, grad_out,
    rows, part, core_got, x_send, x_got, kept, final, sems,
):
    count, cap, width = packed.shape
    depth = width // 2
    me = lax.axis_index("seq")
    e, x, c = me // 4, (me % 4) // 2, me % 2
    own = c * 2 + x
    own_x = c * 2 + 1 - x
    other = (1 - c) * 2 + x
    other_x = (1 - c) * 2 + 1 - x

    def place(e_to, x_to, c_to):
        return {"seq": e_to * 4 + x_to * 2 + c_to}

    core_peer, x_peer = place(e, x, 1 - c), place(e, 1 - x, c)

    def copy(kind, k, source, target, device):
        return pltpu.make_async_remote_copy(
            src_ref=source,
            dst_ref=target,
            send_sem=sems.at[0, kind, k],
            recv_sem=sems.at[1, kind, k],
            device_id=device,
            device_id_type=MESH,
        )

    def block(k):
        return (e + count - k) % count

    def dispatch(k):
        to = (e + k) % count
        return copy(0, k, packed.at[to], rows.at[e, own], place(to, x, c))

    def near(kind, k, section, device):
        piece = rows.at[block(k), section]
        return copy(kind, k, piece, piece, device)

    def core_sum(k):
        f = block(k)
        return copy(4, k, part.at[f, pl.ds((1 - c) * 2, 2)], core_got.at[f], core_peer)

    def x_sum(k):
        f = block(k)
        return copy(5, k, x_send.at[f], x_got.at[f], x_peer)

    def give_back(k, slot):
        f = block(k)
        return copy(6, k, final.at[f], back.at[slot], place(f, x, c))

    barrier = pltpu.get_barrier_semaphore()
    pl.semaphore_signal(barrier, inc=1, device_id=core_peer, device_id_type=MESH)
    pl.semaphore_signal(barrier, inc=1, device_id=x_peer, device_id_type=MESH)

    def greet(k, carry):
        pl.semaphore_signal(
            barrier, inc=1, device_id=place((e + k) % count, x, c), device_id_type=MESH
        )
        return carry

    lax.fori_loop(1, count, greet, 0)
    pl.semaphore_wait(barrier, count + 1)

    def send_first(k, carry):
        dispatch(k).start()
        return carry

    lax.fori_loop(1, count, send_first, 0)
    rows[e, own] = packed[e]
    grad_in[...] = jnp.zeros_like(grad_in)
    grad_out[...] = jnp.zeros_like(grad_out)

    def stage_spread(k):
        f = block(k)

        @pl.when(k > 0)
        def _():
            copy(0, k, packed.at[f], rows.at[f, own], place(f, x, c)).wait_recv()

        near(1, k, own, x_peer).start()
        near(2, k, own, core_peer).start()

    def stage_forward(k):
        near(1, k, own_x, x_peer).wait_recv()
        near(3, k, own_x, core_peer).start()

    def stage_compute(k):
        f = block(k)
        near(2, k, other, core_peer).wait_recv()
        near(3, k, other_x, core_peer).wait_recv()
        values = rows[f].reshape(4 * cap, width)
        normed, grads = values[:, :depth], values[:, depth:]
        pre_act = dot_over(normed, w_in[...], 1, 0)
        hidden_f, slope = swish_parts(pre_act)
        hidden = hidden_f.astype(jnp.bfloat16)
        grad_pre = (dot_over(grads, w_out[...], 1, 1) * slope).astype(jnp.bfloat16)
        part[f, :, :, :depth] = (
            dot_over(hidden, w_out[...], 1, 0).astype(jnp.bfloat16).reshape(4, cap, depth)
        )
        part[f, :, :, depth:] = (
            dot_over(grad_pre, w_in[...], 1, 1).astype(jnp.bfloat16).reshape(4, cap, depth)
        )
        core_sum(k).start()
        grad_out[...] += dot_over(hidden, grads, 0, 0)
        grad_in[...] += dot_over(normed, grad_pre, 0, 0)

    def stage_core(k):
        f = block(k)
        core_sum(k).wait_recv()
        x_send[f] = (
            part[f, own_x].astype(jnp.float32) + core_got[f, 1 - x].astype(jnp.float32)
        ).astype(jnp.bfloat16)
        x_sum(k).start()
        kept[f] = part[f, own].astype(jnp.float32) + core_got[f, x].astype(jnp.float32)

    def stage_back(k):
        f = block(k)
        x_sum(k).wait_recv()
        total = (kept[f] + x_got[f].astype(jnp.float32)).astype(jnp.bfloat16)

        @pl.when(k == 0)
        def _():
            back[e] = total

        @pl.when(k > 0)
        def _():
            final[f] = total
            give_back(k, e).start()

    stages = (
        (4, stage_back),
        (3, stage_core),
        (1, stage_forward),
        (0, stage_spread),
        (2, stage_compute),
    )

    def step(t, carry):
        for lag, stage in stages:
            k = t - lag

            @pl.when((k >= 0) & (k < count))
            def _(stage=stage, k=k):
                stage(k)

        return carry

    lax.fori_loop(0, count + 4, step, 0)

    def finish(k, carry):
        @pl.when(k > 0)
        def _():
            dispatch(k).wait_send()
            give_back(k, e).wait_send()
            give_back(k, (e + k) % count).wait_recv()

        near(1, k, own, x_peer).wait_send()
        near(2, k, own, core_peer).wait_send()
        near(3, k, own_x, core_peer).wait_send()
        core_sum(k).wait_send()
        x_sum(k).wait_send()
        return carry

    lax.fori_loop(0, count, finish, 0)


def moe(packed, w_in, w_out):
    count, cap, width = packed.shape
    vmem = pl.BlockSpec(memory_space=pltpu.VMEM)
    half = jnp.bfloat16
    return pl.pallas_call(
        moe_kernel,
        out_shape=(
            jax.ShapeDtypeStruct(packed.shape, half),
            jax.ShapeDtypeStruct(w_in.shape, jnp.float32),
            jax.ShapeDtypeStruct(w_out.shape, jnp.float32),
        ),
        in_specs=[vmem] * 3,
        out_specs=(vmem,) * 3,
        scratch_shapes=[
            pltpu.VMEM((count, 4, cap, width), half),
            pltpu.VMEM((count, 4, cap, width), half),
            pltpu.VMEM((count, 2, cap, width), half),
            pltpu.VMEM((count, cap, width), half),
            pltpu.VMEM((count, cap, width), half),
            pltpu.VMEM((count, cap, width), jnp.float32),
            pltpu.VMEM((count, cap, width), half),
            pltpu.SemaphoreType.DMA((2, 7, count)),
        ],
        compiler_params=pltpu.CompilerParams(
            collective_id=0, has_side_effects=True, vmem_limit_bytes=56 * 2**20
        ),
    )(packed, w_in, w_out)


def sum_kernel(terms, totals, near_got, near_sum, far_got, sems):
    seq_size = lax.axis_size("seq")
    seq, dp = lax.axis_index("seq"), lax.axis_index("dp")
    groups = terms.shape[1]
    m, h = seq % 4, dp * (seq_size // 4) + seq // 4

    def mate(j):
        return {"dp": dp, "seq": seq // 4 * 4 + (m + j) % 4}

    def peer(j):
        number = (h + j) % groups * 4 + m
        return {"dp": number // seq_size, "seq": number % seq_size}

    def copy(phase, j, source, target, device):
        return pltpu.make_async_remote_copy(
            src_ref=source,
            dst_ref=target,
            send_sem=sems.at[phase, 0, j],
            recv_sem=sems.at[phase, 1, j],
            device_id=device,
            device_id_type=MESH,
        )

    def every(size, action):
        def one(j, carry):
            action(j)
            return carry

        lax.fori_loop(1, size, one, 0)

    def behind_m(j):
        return (m + 4 - j) % 4

    def behind_h(j):
        return (h + groups - j) % groups

    def near_in(j, slot):
        return copy(0, j, terms.at[(m + j) % 4], near_got.at[slot], mate(j))

    def far_in(j, slot):
        return copy(1, j, near_sum.at[(h + j) % groups], far_got.at[slot], peer(j))

    def far_out(j, slot):
        return copy(2, j, totals.at[m, h], totals.at[m, slot], peer(j))

    def near_out(j, slot):
        return copy(3, j, totals.at[m], totals.at[slot], mate(j))

    barrier = pltpu.get_barrier_semaphore()

    def greet(device):
        pl.semaphore_signal(barrier, inc=1, device_id=device, device_id_type=MESH)

    every(4, lambda j: greet(mate(j)))
    every(groups, lambda j: greet(peer(j)))
    pl.semaphore_wait(barrier, groups + 2)
    every(4, lambda j: near_in(j, m).start())
    near_got[m] = terms[m]
    every(4, lambda j: near_in(j, behind_m(j)).wait_recv())
    near_sum[...] = jnp.sum(near_got[...], axis=0)
    every(groups, lambda j: far_in(j, h).start())
    far_got[h] = near_sum[h]
    every(groups, lambda j: far_in(j, behind_h(j)).wait_recv())
    totals[m, h] = jnp.sum(far_got[...], axis=0)
    every(groups, lambda j: far_out(j, h).start())
    every(groups, lambda j: far_out(j, behind_h(j)).wait_recv())
    every(4, lambda j: near_out(j, m).start())
    every(4, lambda j: near_out(j, behind_m(j)).wait_recv())
    every(4, lambda j: near_in(j, m).wait_send())
    every(groups, lambda j: far_in(j, h).wait_send())
    every(groups, lambda j: far_out(j, h).wait_send())
    every(4, lambda j: near_out(j, m).wait_send())


def sum_everywhere(rows):
    groups = lax.axis_size("seq") * lax.axis_size("dp") // 4
    size = rows.size
    tall = -(-size // (groups * 4 * 1024)) * 8
    padded = jnp.pad(rows.reshape(-1), (0, groups * 4 * tall * 128 - size)).reshape(
        4, groups, tall, 128
    )
    vmem = pl.BlockSpec(memory_space=pltpu.VMEM)
    totals = pl.pallas_call(
        sum_kernel,
        out_shape=jax.ShapeDtypeStruct(padded.shape, jnp.float32),
        in_specs=[vmem],
        out_specs=vmem,
        scratch_shapes=[
            pltpu.VMEM(padded.shape, jnp.float32),
            pltpu.VMEM(padded.shape[1:], jnp.float32),
            pltpu.VMEM(padded.shape[1:], jnp.float32),
            pltpu.SemaphoreType.DMA((4, 2, max(groups, 4))),
        ],
        compiler_params=pltpu.CompilerParams(collective_id=1, has_side_effects=True),
    )(padded)
    return totals.reshape(-1)[:size].reshape(rows.shape)


def body(frames, kernel, norm_gain, router, experts, w_in, w_out, cotangent):
    inputs_dev = frames[0]
    row_count = inputs_dev.shape[0]
    width = inputs_dev.shape[1]
    length = kernel.shape[0]
    half_width = length // 2
    expert_count = router.shape[1]
    top_count = experts.shape[2]
    capacity = 2 * row_count * top_count // expert_count
    in_weights = w_in[0]
    out_weights = w_out[0]
    padded = padded_2(inputs_dev, (("seq", 0),), half_width)
    summed = inputs_dev.astype(jnp.float32) + conv_forward(padded, kernel, row_count)
    normed_b = normalize(summed, norm_gain).astype(jnp.bfloat16)
    choice_ids = experts[0]
    gate_one, gate_two, pick_diff = gate_values(
        normed_b, router, choice_ids[:, 0], choice_ids[:, 1]
    )
    flat_ids = choice_ids.reshape(-1)
    slot_index = slot_numbers(flat_ids, expert_count)
    position = flat_ids * capacity + slot_index
    dispatch_table = (
        lax.broadcasted_iota(jnp.int32, (expert_count * capacity, flat_ids.shape[0]), 0)
        == position[None, :]
    ).astype(jnp.bfloat16)

    def pack(values):
        return jnp.dot(dispatch_table, values, preferred_element_type=jnp.float32).astype(
            jnp.bfloat16
        )

    repeated = jnp.repeat(normed_b, top_count, axis=0)
    upstream = cotangent[0].astype(jnp.float32)
    grad_assigned = jnp.stack([gate_one[:, None] * upstream, gate_two[:, None] * upstream], axis=1)
    grad_values = grad_assigned.reshape(row_count * top_count, width).astype(jnp.bfloat16)
    packed = pack(jnp.concatenate([repeated, grad_values], axis=1))
    back, in_term, out_term = moe(
        packed.reshape(expert_count, capacity, 2 * width), in_weights, out_weights
    )
    back = back.reshape(expert_count * capacity, 2 * width)
    assigned = dot_over(dispatch_table, back[:, :width], 0, 0).reshape(
        row_count, top_count, width
    )
    out_one = assigned[:, 0]
    out_two = assigned[:, 1]
    mixed = (summed + gate_one[:, None] * out_one + gate_two[:, None] * out_two).astype(
        jnp.bfloat16
    )
    both = jnp.sum(dispatch_table.reshape(-1, row_count, top_count), axis=2)
    normed_grads = dot_over(both, back[:, width:], 0, 0)
    router_term, normed_term = gate_backward(
        upstream, out_one, out_two, gate_one, gate_two, pick_diff, normed_b, router
    )
    pullback = jax.vjp(normalize, summed, norm_gain)[1]
    summed_grad, gain_term = pullback(normed_grads + normed_term)
    upstream_total = upstream + summed_grad
    padded_grad = padded_2(upstream_total.astype(jnp.bfloat16), (("seq", 0),), half_width).astype(
        upstream_total.dtype
    )
    grad_frames = (upstream_total + conv_transpose(padded_grad, kernel, row_count)).astype(
        jnp.bfloat16
    )
    kernel_term = kernel_terms(padded, upstream_total, length, row_count)
    sums = sum_everywhere(
        jnp.concatenate([kernel_term, gain_term[None], router_term.T], axis=0)
    )
    grad_kernel, grad_gain = sums[:length], sums[length]
    grad_router = sums[length + 1 :].T
    grad_in, grad_out = in_term, out_term
    if lax.axis_size("dp") > 1:
        grad_in, grad_out = (
            lax.psum(in_term.astype(jnp.bfloat16), "dp").astype(jnp.float32),
            lax.psum(out_term.astype(jnp.bfloat16), "dp").astype(jnp.float32),
        )
    return (
        mixed[None],
        grad_frames[None],
        grad_kernel,
        grad_gain,
        grad_router,
        grad_in[None],
        grad_out[None],
    )


def solution(mesh):
    return jax.shard_map(
        body,
        mesh=mesh,
        in_specs=(
            P("dp", "seq", None),
            P(),
            P(),
            P(),
            P("dp", "seq", None),
            P("seq", None, None),
            P("seq", None, None),
            P("dp", "seq", None),
        ),
        out_specs=(
            P("dp", "seq", None),
            P("dp", "seq", None),
            P(),
            P(),
            P(),
            P("seq", None, None),
            P("seq", None, None),
        ),
        check_vma=False,
    )
```

```python
import jax
import jax.numpy as jnp
from jax import lax
from jax.experimental import pallas as pl
from jax.experimental.pallas import tpu as pltpu
from jax.sharding import PartitionSpec as P

MESH = pl.DeviceIdType.MESH

eps = 1e-06


def padded_2(shard, sides, width):
    for axis, dim in sides:
        size, length = (lax.axis_size(axis), shard.shape[dim])
        up = [(i, (i + 1) % size) for i in range(size - 1)]
        down = [(j, i) for i, j in up]
        last = lax.slice_in_dim(shard, length - width, length, axis=dim)
        initial = lax.slice_in_dim(shard, 0, width, axis=dim)
        before = lax.ppermute(last, axis, up)
        after = lax.ppermute(initial, axis, down)
        shard = jnp.concatenate([before, shard, after], axis=dim)
    return shard


def conv_norm_kernel(padded, kernel, gain, summed, normed, wide):
    row_count, width = summed.shape
    length = kernel.shape[0]
    wide[: padded.shape[0]] = padded[...].astype(jnp.float32)

    def columns(i):
        return pl.ds(pl.multiple_of(i * 128, 128), 128)

    def convolve(i, square):
        at = columns(i)
        total = jnp.zeros((row_count, 128), jnp.float32)
        for offset in range(length):
            weight = kernel[offset : offset + 1, at].astype(jnp.float32)
            total = total + weight * wide[offset : offset + row_count, at]
        total = wide[length // 2 : length // 2 + row_count, at] + total
        summed[:, at] = total
        return square + total * total

    square = lax.fori_loop(
        0, width // 128, convolve, jnp.zeros((row_count, 128), jnp.float32)
    )
    scale = lax.rsqrt(jnp.sum(square, axis=1, keepdims=True) / width + eps)

    def apply(i, carry):
        at = columns(i)
        normed[:, at] = (summed[:, at] * scale * gain[:, at]).astype(jnp.bfloat16)
        return carry

    lax.fori_loop(0, width // 128, apply, 0)


def conv_norm(padded, kernel, norm_gain, row_count):
    width = padded.shape[1]
    tall = -(-padded.shape[0] // 16) * 16
    vmem = pl.BlockSpec(memory_space=pltpu.VMEM)
    return pl.pallas_call(
        conv_norm_kernel,
        out_shape=(
            jax.ShapeDtypeStruct((row_count, width), jnp.float32),
            jax.ShapeDtypeStruct((row_count, width), jnp.bfloat16),
        ),
        in_specs=[vmem] * 3,
        out_specs=(vmem,) * 2,
        scratch_shapes=[pltpu.VMEM((tall, width), jnp.float32)],
        compiler_params=pltpu.CompilerParams(vmem_limit_bytes=12 * 2**20),
    )(
        jnp.pad(padded, ((0, tall - padded.shape[0]), (0, 0))),
        kernel.astype(jnp.float32),
        norm_gain[None],
    )


def conv_transpose(padded, kernel, row_count):
    length = kernel.shape[0]
    summed = jnp.zeros((row_count, padded.shape[1]), jnp.float32)
    for offset in range(length):
        start = length - 1 - offset
        summed = summed + kernel[offset].astype(jnp.float32) * padded[start : start + row_count]
    return summed


def kernel_terms(padded, upstream, length, row_count):
    return jnp.stack(
        [
            jnp.sum(padded[offset : offset + row_count].astype(jnp.float32) * upstream, axis=0)
            for offset in range(length)
        ]
    )


def normalize(summed, norm_gain):
    square = jnp.mean(summed * summed, axis=-1, keepdims=True)
    return summed * lax.rsqrt(square + eps) * norm_gain


def slot_numbers(expert_ids, expert_count):
    onehot = (expert_ids[:, None] == jnp.arange(expert_count, dtype=jnp.int32)[None, :]).astype(
        jnp.int32
    )
    ranks = jnp.cumsum(onehot, axis=0) - onehot
    return jnp.sum(ranks * onehot, axis=1)


def gate_values(normed_b, router, first_ids, second_ids):
    logits = jnp.dot(normed_b, router, preferred_element_type=jnp.float32)
    columns = jnp.arange(router.shape[1], dtype=jnp.int32)[None, :]
    pick_diff = (first_ids[:, None] == columns).astype(jnp.float32) - (
        second_ids[:, None] == columns
    ).astype(jnp.float32)
    gate_one = jax.nn.sigmoid(jnp.sum(logits * pick_diff, axis=1))
    return (gate_one, 1.0 - gate_one, pick_diff)


def swish_parts(pre_act):
    squash = jax.nn.sigmoid(pre_act)
    return (pre_act * squash, squash * (1.0 + pre_act * (1.0 - squash)))


def gate_backward(upstream, out_one, out_two, gate_one, gate_two, pick_diff, normed_b, router):
    grad_gap = (
        (jnp.sum(upstream * out_one, axis=1) - jnp.sum(upstream * out_two, axis=1))
        * gate_one
        * gate_two
    )
    grad_logits = (grad_gap[:, None] * pick_diff).astype(jnp.bfloat16)
    router_term = jnp.dot(normed_b.T, grad_logits, preferred_element_type=jnp.float32)
    normed_term = jnp.dot(grad_logits, router.T, preferred_element_type=jnp.float32)
    return (router_term, normed_term)


def dot_over(left, right, left_dim, right_dim):
    return lax.dot_general(
        left, right, (((left_dim,), (right_dim,)), ((), ())), preferred_element_type=jnp.float32
    )


def moe_kernel(
    packed, w_in, w_out, back, grad_in, grad_out,
    rows, part, core_got, x_send, x_got, kept, final, sems,
):
    count, cap, width = packed.shape
    depth = width // 2
    me = lax.axis_index("seq")
    e, x, c = me // 4, (me % 4) // 2, me % 2
    own = c * 2 + x
    own_x = c * 2 + 1 - x
    other = (1 - c) * 2 + x
    other_x = (1 - c) * 2 + 1 - x

    def place(e_to, x_to, c_to):
        return {"seq": e_to * 4 + x_to * 2 + c_to}

    core_peer, x_peer = place(e, x, 1 - c), place(e, 1 - x, c)

    def copy(kind, k, source, target, device):
        return pltpu.make_async_remote_copy(
            src_ref=source,
            dst_ref=target,
            send_sem=sems.at[0, kind, k],
            recv_sem=sems.at[1, kind, k],
            device_id=device,
            device_id_type=MESH,
        )

    def block(k):
        return (e + count - k) % count

    def dispatch(k):
        to = (e + k) % count
        return copy(0, k, packed.at[to], rows.at[e, own], place(to, x, c))

    def near(kind, k, section, device):
        piece = rows.at[block(k), section]
        return copy(kind, k, piece, piece, device)

    def core_sum(k):
        f = block(k)
        return copy(4, k, part.at[f, pl.ds((1 - c) * 2, 2)], core_got.at[f], core_peer)

    def x_sum(k):
        f = block(k)
        return copy(5, k, x_send.at[f], x_got.at[f], x_peer)

    def give_back(k, slot):
        f = block(k)
        return copy(6, k, final.at[f], back.at[slot], place(f, x, c))

    barrier = pltpu.get_barrier_semaphore()
    pl.semaphore_signal(barrier, inc=1, device_id=core_peer, device_id_type=MESH)
    pl.semaphore_signal(barrier, inc=1, device_id=x_peer, device_id_type=MESH)

    def greet(k, carry):
        pl.semaphore_signal(
            barrier, inc=1, device_id=place((e + k) % count, x, c), device_id_type=MESH
        )
        return carry

    lax.fori_loop(1, count, greet, 0)
    pl.semaphore_wait(barrier, count + 1)

    def send_first(k, carry):
        dispatch(k).start()
        return carry

    ahead = min(4, count)
    lax.fori_loop(1, ahead, send_first, 0)
    rows[e, own] = packed[e]
    grad_in[...] = jnp.zeros_like(grad_in)
    grad_out[...] = jnp.zeros_like(grad_out)

    def stage_spread(k):
        f = block(k)

        @pl.when(k > 0)
        def _():
            copy(0, k, packed.at[f], rows.at[f, own], place(f, x, c)).wait_recv()

        near(1, k, own, x_peer).start()
        near(2, k, own, core_peer).start()

        @pl.when(k + ahead < count)
        def _():
            dispatch(k + ahead).start()

    def stage_forward(k):
        near(1, k, own_x, x_peer).wait_recv()
        near(3, k, own_x, core_peer).start()

    def stage_compute(k):
        f = block(k)
        near(2, k, other, core_peer).wait_recv()
        near(3, k, other_x, core_peer).wait_recv()
        values = rows[f].reshape(4 * cap, width)
        normed, grads = values[:, :depth], values[:, depth:]
        pre_act = dot_over(normed, w_in[...], 1, 0)
        hidden_f, slope = swish_parts(pre_act)
        hidden = hidden_f.astype(jnp.bfloat16)
        grad_pre = (dot_over(grads, w_out[...], 1, 1) * slope).astype(jnp.bfloat16)
        part[f, :, :, :depth] = (
            dot_over(hidden, w_out[...], 1, 0).astype(jnp.bfloat16).reshape(4, cap, depth)
        )
        part[f, :, :, depth:] = (
            dot_over(grad_pre, w_in[...], 1, 1).astype(jnp.bfloat16).reshape(4, cap, depth)
        )
        core_sum(k).start()
        grad_out[...] += dot_over(hidden, grads, 0, 0)
        grad_in[...] += dot_over(normed, grad_pre, 0, 0)

    def stage_core(k):
        f = block(k)
        core_sum(k).wait_recv()
        x_send[f] = (
            part[f, own_x].astype(jnp.float32) + core_got[f, 1 - x].astype(jnp.float32)
        ).astype(jnp.bfloat16)
        x_sum(k).start()
        kept[f] = part[f, own].astype(jnp.float32) + core_got[f, x].astype(jnp.float32)

    def stage_back(k):
        f = block(k)
        x_sum(k).wait_recv()
        total = (kept[f] + x_got[f].astype(jnp.float32)).astype(jnp.bfloat16)

        @pl.when(k == 0)
        def _():
            back[e] = total

        @pl.when(k > 0)
        def _():
            final[f] = total
            give_back(k, e).start()

    stages = (
        (4, stage_back),
        (3, stage_core),
        (2, stage_compute),
        (1, stage_forward),
        (0, stage_spread),
    )

    def step(t, carry):
        for lag, stage in stages:
            k = t - lag

            @pl.when((k >= 0) & (k < count))
            def _(stage=stage, k=k):
                stage(k)

        return carry

    lax.fori_loop(0, count + 4, step, 0)

    def finish(k, carry):
        @pl.when(k > 0)
        def _():
            dispatch(k).wait_send()
            give_back(k, e).wait_send()
            give_back(k, (e + k) % count).wait_recv()

        near(1, k, own, x_peer).wait_send()
        near(2, k, own, core_peer).wait_send()
        near(3, k, own_x, core_peer).wait_send()
        core_sum(k).wait_send()
        x_sum(k).wait_send()
        return carry

    lax.fori_loop(0, count, finish, 0)


def moe(packed, w_in, w_out):
    count, cap, width = packed.shape
    vmem = pl.BlockSpec(memory_space=pltpu.VMEM)
    half = jnp.bfloat16
    return pl.pallas_call(
        moe_kernel,
        out_shape=(
            jax.ShapeDtypeStruct(packed.shape, half),
            jax.ShapeDtypeStruct(w_in.shape, jnp.float32),
            jax.ShapeDtypeStruct(w_out.shape, jnp.float32),
        ),
        in_specs=[vmem] * 3,
        out_specs=(vmem,) * 3,
        scratch_shapes=[
            pltpu.VMEM((count, 4, cap, width), half),
            pltpu.VMEM((count, 4, cap, width), half),
            pltpu.VMEM((count, 2, cap, width), half),
            pltpu.VMEM((count, cap, width), half),
            pltpu.VMEM((count, cap, width), half),
            pltpu.VMEM((count, cap, width), jnp.float32),
            pltpu.VMEM((count, cap, width), half),
            pltpu.SemaphoreType.DMA((2, 7, count)),
        ],
        compiler_params=pltpu.CompilerParams(
            collective_id=0, has_side_effects=True, vmem_limit_bytes=56 * 2**20
        ),
    )(packed, w_in, w_out)


def sum_kernel(terms, totals, near_got, near_sum, far_got, sems):
    seq_size = lax.axis_size("seq")
    seq, dp = lax.axis_index("seq"), lax.axis_index("dp")
    groups = terms.shape[1]
    m, h = seq % 4, dp * (seq_size // 4) + seq // 4

    def mate(j):
        return {"dp": dp, "seq": seq // 4 * 4 + (m + j) % 4}

    def peer(j):
        number = (h + j) % groups * 4 + m
        return {"dp": number // seq_size, "seq": number % seq_size}

    def copy(phase, j, source, target, device):
        return pltpu.make_async_remote_copy(
            src_ref=source,
            dst_ref=target,
            send_sem=sems.at[phase, 0, j],
            recv_sem=sems.at[phase, 1, j],
            device_id=device,
            device_id_type=MESH,
        )

    def every(size, action):
        def one(j, carry):
            action(j)
            return carry

        lax.fori_loop(1, size, one, 0)

    def behind_m(j):
        return (m + 4 - j) % 4

    def behind_h(j):
        return (h + groups - j) % groups

    def near_in(j, slot):
        return copy(0, j, terms.at[(m + j) % 4], near_got.at[slot], mate(j))

    def far_in(j, slot):
        return copy(1, j, near_sum.at[(h + j) % groups], far_got.at[slot], peer(j))

    def far_out(j, slot):
        return copy(2, j, totals.at[m, h], totals.at[m, slot], peer(j))

    def near_out(j, slot):
        return copy(3, j, totals.at[m], totals.at[slot], mate(j))

    barrier = pltpu.get_barrier_semaphore()

    def greet(device):
        pl.semaphore_signal(barrier, inc=1, device_id=device, device_id_type=MESH)

    every(4, lambda j: greet(mate(j)))
    every(groups, lambda j: greet(peer(j)))
    pl.semaphore_wait(barrier, groups + 2)
    every(4, lambda j: near_in(j, m).start())
    near_got[m] = terms[m]
    every(4, lambda j: near_in(j, behind_m(j)).wait_recv())
    near_sum[...] = jnp.sum(near_got[...], axis=0)
    every(groups, lambda j: far_in(j, h).start())
    far_got[h] = near_sum[h]
    every(groups, lambda j: far_in(j, behind_h(j)).wait_recv())
    totals[m, h] = jnp.sum(far_got[...], axis=0)
    every(groups, lambda j: far_out(j, h).start())
    every(groups, lambda j: far_out(j, behind_h(j)).wait_recv())
    every(4, lambda j: near_out(j, m).start())
    every(4, lambda j: near_out(j, behind_m(j)).wait_recv())
    every(4, lambda j: near_in(j, m).wait_send())
    every(groups, lambda j: far_in(j, h).wait_send())
    every(groups, lambda j: far_out(j, h).wait_send())
    every(4, lambda j: near_out(j, m).wait_send())


def sum_everywhere(rows):
    groups = lax.axis_size("seq") * lax.axis_size("dp") // 4
    size = rows.size
    tall = -(-size // (groups * 4 * 1024)) * 8
    padded = jnp.pad(rows.reshape(-1), (0, groups * 4 * tall * 128 - size)).reshape(
        4, groups, tall, 128
    )
    vmem = pl.BlockSpec(memory_space=pltpu.VMEM)
    totals = pl.pallas_call(
        sum_kernel,
        out_shape=jax.ShapeDtypeStruct(padded.shape, jnp.float32),
        in_specs=[vmem],
        out_specs=vmem,
        scratch_shapes=[
            pltpu.VMEM(padded.shape, jnp.float32),
            pltpu.VMEM(padded.shape[1:], jnp.float32),
            pltpu.VMEM(padded.shape[1:], jnp.float32),
            pltpu.SemaphoreType.DMA((4, 2, max(groups, 4))),
        ],
        compiler_params=pltpu.CompilerParams(collective_id=1, has_side_effects=True),
    )(padded)
    return totals.reshape(-1)[:size].reshape(rows.shape)


def body(frames, kernel, norm_gain, router, experts, w_in, w_out, cotangent):
    inputs_dev = frames[0]
    row_count = inputs_dev.shape[0]
    width = inputs_dev.shape[1]
    length = kernel.shape[0]
    half_width = length // 2
    expert_count = router.shape[1]
    top_count = experts.shape[2]
    capacity = 2 * row_count * top_count // expert_count
    in_weights = w_in[0]
    out_weights = w_out[0]
    padded = padded_2(inputs_dev, (("seq", 0),), half_width)
    summed, normed_b = conv_norm(padded, kernel, norm_gain, row_count)
    choice_ids = experts[0]
    gate_one, gate_two, pick_diff = gate_values(
        normed_b, router, choice_ids[:, 0], choice_ids[:, 1]
    )
    flat_ids = choice_ids.reshape(-1)
    slot_index = slot_numbers(flat_ids, expert_count)
    position = flat_ids * capacity + slot_index
    dispatch_table = (
        lax.broadcasted_iota(jnp.int32, (expert_count * capacity, flat_ids.shape[0]), 0)
        == position[None, :]
    ).astype(jnp.bfloat16)

    def pack(values):
        return jnp.dot(dispatch_table, values, preferred_element_type=jnp.float32).astype(
            jnp.bfloat16
        )

    repeated = jnp.repeat(normed_b, top_count, axis=0)
    upstream = cotangent[0].astype(jnp.float32)
    grad_assigned = jnp.stack([gate_one[:, None] * upstream, gate_two[:, None] * upstream], axis=1)
    grad_values = grad_assigned.reshape(row_count * top_count, width).astype(jnp.bfloat16)
    packed = pack(jnp.concatenate([repeated, grad_values], axis=1))
    back, in_term, out_term = moe(
        packed.reshape(expert_count, capacity, 2 * width), in_weights, out_weights
    )
    back = back.reshape(expert_count * capacity, 2 * width)
    assigned = dot_over(dispatch_table, back[:, :width], 0, 0).reshape(
        row_count, top_count, width
    )
    out_one = assigned[:, 0]
    out_two = assigned[:, 1]
    mixed = (summed + gate_one[:, None] * out_one + gate_two[:, None] * out_two).astype(
        jnp.bfloat16
    )
    both = jnp.sum(dispatch_table.reshape(-1, row_count, top_count), axis=2)
    normed_grads = dot_over(both, back[:, width:], 0, 0)
    router_term, normed_term = gate_backward(
        upstream, out_one, out_two, gate_one, gate_two, pick_diff, normed_b, router
    )
    pullback = jax.vjp(normalize, summed, norm_gain)[1]
    summed_grad, gain_term = pullback(normed_grads + normed_term)
    upstream_total = upstream + summed_grad
    padded_grad = padded_2(upstream_total.astype(jnp.bfloat16), (("seq", 0),), half_width).astype(
        upstream_total.dtype
    )
    grad_frames = (upstream_total + conv_transpose(padded_grad, kernel, row_count)).astype(
        jnp.bfloat16
    )
    kernel_term = kernel_terms(padded, upstream_total, length, row_count)
    sums = sum_everywhere(
        jnp.concatenate([kernel_term, gain_term[None], router_term.T], axis=0)
    )
    grad_kernel, grad_gain = sums[:length], sums[length]
    grad_router = sums[length + 1 :].T
    grad_in, grad_out = in_term, out_term
    if lax.axis_size("dp") > 1:
        grad_in, grad_out = (
            lax.psum(in_term.astype(jnp.bfloat16), "dp").astype(jnp.float32),
            lax.psum(out_term.astype(jnp.bfloat16), "dp").astype(jnp.float32),
        )
    return (
        mixed[None],
        grad_frames[None],
        grad_kernel,
        grad_gain,
        grad_router,
        grad_in[None],
        grad_out[None],
    )


def solution(mesh):
    return jax.shard_map(
        body,
        mesh=mesh,
        in_specs=(
            P("dp", "seq", None),
            P(),
            P(),
            P(),
            P("dp", "seq", None),
            P("seq", None, None),
            P("seq", None, None),
            P("dp", "seq", None),
        ),
        out_specs=(
            P("dp", "seq", None),
            P("dp", "seq", None),
            P(),
            P(),
            P(),
            P("seq", None, None),
            P("seq", None, None),
        ),
        check_vma=False,
    )
```

```python
import jax
import jax.numpy as jnp
from jax import lax
from jax.experimental import pallas as pl
from jax.experimental.pallas import tpu as pltpu
from jax.sharding import PartitionSpec as P

MESH = pl.DeviceIdType.MESH

eps = 1e-06


def padded_2(shard, sides, width):
    for axis, dim in sides:
        size, length = (lax.axis_size(axis), shard.shape[dim])
        up = [(i, (i + 1) % size) for i in range(size - 1)]
        down = [(j, i) for i, j in up]
        last = lax.slice_in_dim(shard, length - width, length, axis=dim)
        initial = lax.slice_in_dim(shard, 0, width, axis=dim)
        before = lax.ppermute(last, axis, up)
        after = lax.ppermute(initial, axis, down)
        shard = jnp.concatenate([before, shard, after], axis=dim)
    return shard


def conv_norm_kernel(padded, kernel, gain, summed, normed, wide):
    row_count, width = summed.shape
    length = kernel.shape[0]
    wide[: padded.shape[0]] = padded[...].astype(jnp.float32)

    def columns(i):
        return pl.ds(pl.multiple_of(i * 128, 128), 128)

    def convolve(i, square):
        at = columns(i)
        total = jnp.zeros((row_count, 128), jnp.float32)
        for offset in range(length):
            weight = kernel[offset : offset + 1, at].astype(jnp.float32)
            total = total + weight * wide[offset : offset + row_count, at]
        total = wide[length // 2 : length // 2 + row_count, at] + total
        summed[:, at] = total
        return square + total * total

    square = lax.fori_loop(
        0, width // 128, convolve, jnp.zeros((row_count, 128), jnp.float32)
    )
    scale = lax.rsqrt(jnp.sum(square, axis=1, keepdims=True) / width + eps)

    def apply(i, carry):
        at = columns(i)
        normed[:, at] = (summed[:, at] * scale * gain[:, at]).astype(jnp.bfloat16)
        return carry

    lax.fori_loop(0, width // 128, apply, 0)


def conv_norm(padded, kernel, norm_gain, row_count):
    width = padded.shape[1]
    tall = -(-padded.shape[0] // 16) * 16
    vmem = pl.BlockSpec(memory_space=pltpu.VMEM)
    return pl.pallas_call(
        conv_norm_kernel,
        out_shape=(
            jax.ShapeDtypeStruct((row_count, width), jnp.float32),
            jax.ShapeDtypeStruct((row_count, width), jnp.bfloat16),
        ),
        in_specs=[vmem] * 3,
        out_specs=(vmem,) * 2,
        scratch_shapes=[pltpu.VMEM((tall, width), jnp.float32)],
        compiler_params=pltpu.CompilerParams(vmem_limit_bytes=12 * 2**20),
    )(
        jnp.pad(padded, ((0, tall - padded.shape[0]), (0, 0))),
        kernel.astype(jnp.float32),
        norm_gain[None],
    )


def conv_transpose(padded, kernel, row_count):
    length = kernel.shape[0]
    summed = jnp.zeros((row_count, padded.shape[1]), jnp.float32)
    for offset in range(length):
        start = length - 1 - offset
        summed = summed + kernel[offset].astype(jnp.float32) * padded[start : start + row_count]
    return summed


def kernel_terms(padded, upstream, length, row_count):
    return jnp.stack(
        [
            jnp.sum(padded[offset : offset + row_count].astype(jnp.float32) * upstream, axis=0)
            for offset in range(length)
        ]
    )


def normalize(summed, norm_gain):
    square = jnp.mean(summed * summed, axis=-1, keepdims=True)
    return summed * lax.rsqrt(square + eps) * norm_gain


def slot_numbers(expert_ids, expert_count):
    onehot = (expert_ids[:, None] == jnp.arange(expert_count, dtype=jnp.int32)[None, :]).astype(
        jnp.int32
    )
    ranks = jnp.cumsum(onehot, axis=0) - onehot
    return jnp.sum(ranks * onehot, axis=1)


def gate_values(normed_b, router, first_ids, second_ids):
    logits = jnp.dot(normed_b, router, preferred_element_type=jnp.float32)
    columns = jnp.arange(router.shape[1], dtype=jnp.int32)[None, :]
    pick_diff = (first_ids[:, None] == columns).astype(jnp.float32) - (
        second_ids[:, None] == columns
    ).astype(jnp.float32)
    gate_one = jax.nn.sigmoid(jnp.sum(logits * pick_diff, axis=1))
    return (gate_one, 1.0 - gate_one, pick_diff)


def swish_parts(pre_act):
    squash = jax.nn.sigmoid(pre_act)
    return (pre_act * squash, squash * (1.0 + pre_act * (1.0 - squash)))


def gate_backward(upstream, out_one, out_two, gate_one, gate_two, pick_diff, normed_b, router):
    grad_gap = (
        (jnp.sum(upstream * out_one, axis=1) - jnp.sum(upstream * out_two, axis=1))
        * gate_one
        * gate_two
    )
    grad_logits = (grad_gap[:, None] * pick_diff).astype(jnp.bfloat16)
    router_term = jnp.dot(normed_b.T, grad_logits, preferred_element_type=jnp.float32)
    normed_term = jnp.dot(grad_logits, router.T, preferred_element_type=jnp.float32)
    return (router_term, normed_term)


def dot_over(left, right, left_dim, right_dim):
    return lax.dot_general(
        left, right, (((left_dim,), (right_dim,)), ((), ())), preferred_element_type=jnp.float32
    )


def moe_kernel(
    packed, w_in, w_out, back, grad_in, grad_out,
    rows, part, core_got, x_send, x_got, kept, final, sems,
):
    count, cap, width = packed.shape
    depth = width // 2
    me = lax.axis_index("seq")
    e, x, c = me // 4, (me % 4) // 2, me % 2
    own = c * 2 + x
    own_x = c * 2 + 1 - x
    other = (1 - c) * 2 + x
    other_x = (1 - c) * 2 + 1 - x

    def place(e_to, x_to, c_to):
        return {"seq": e_to * 4 + x_to * 2 + c_to}

    core_peer, x_peer = place(e, x, 1 - c), place(e, 1 - x, c)

    def copy(kind, k, source, target, device):
        return pltpu.make_async_remote_copy(
            src_ref=source,
            dst_ref=target,
            send_sem=sems.at[0, kind, k],
            recv_sem=sems.at[1, kind, k],
            device_id=device,
            device_id_type=MESH,
        )

    def block(k):
        return (e + count - k) % count

    def dispatch(k):
        to = (e + k) % count
        return copy(0, k, packed.at[to], rows.at[e, own], place(to, x, c))

    def near(kind, k, section, device):
        piece = rows.at[block(k), section]
        return copy(kind, k, piece, piece, device)

    def core_sum(k):
        f = block(k)
        return copy(4, k, part.at[f, pl.ds((1 - c) * 2, 2)], core_got.at[f], core_peer)

    def x_sum(k):
        f = block(k)
        return copy(5, k, x_send.at[f], x_got.at[f], x_peer)

    def give_back(k, slot):
        f = block(k)
        return copy(6, k, final.at[f], back.at[slot], place(f, x, c))

    barrier = pltpu.get_barrier_semaphore()
    pl.semaphore_signal(barrier, inc=1, device_id=core_peer, device_id_type=MESH)
    pl.semaphore_signal(barrier, inc=1, device_id=x_peer, device_id_type=MESH)

    def greet(k, carry):
        pl.semaphore_signal(
            barrier, inc=1, device_id=place((e + k) % count, x, c), device_id_type=MESH
        )
        return carry

    lax.fori_loop(1, count, greet, 0)
    pl.semaphore_wait(barrier, count + 1)

    def send_first(k, carry):
        dispatch(k).start()
        return carry

    ahead = min(4, count)
    lax.fori_loop(1, ahead, send_first, 0)
    rows[e, own] = packed[e]
    grad_in[...] = jnp.zeros_like(grad_in)
    grad_out[...] = jnp.zeros_like(grad_out)

    def stage_spread(k):
        f = block(k)

        @pl.when(k > 0)
        def _():
            copy(0, k, packed.at[f], rows.at[f, own], place(f, x, c)).wait_recv()

        near(1, k, own, x_peer).start()
        near(2, k, own, core_peer).start()

        @pl.when(k + ahead < count)
        def _():
            dispatch(k + ahead).start()

    def stage_forward(k):
        near(1, k, own_x, x_peer).wait_recv()
        near(3, k, own_x, core_peer).start()

    def stage_compute(k):
        f = block(k)
        near(2, k, other, core_peer).wait_recv()
        near(3, k, other_x, core_peer).wait_recv()
        values = rows[f].reshape(4 * cap, width)
        normed, grads = values[:, :depth], values[:, depth:]
        pre_act = dot_over(normed, w_in[...], 1, 0)
        hidden_f, slope = swish_parts(pre_act)
        hidden = hidden_f.astype(jnp.bfloat16)
        grad_pre = (dot_over(grads, w_out[...], 1, 1) * slope).astype(jnp.bfloat16)
        part[f, :, :, :depth] = (
            dot_over(hidden, w_out[...], 1, 0).astype(jnp.bfloat16).reshape(4, cap, depth)
        )
        part[f, :, :, depth:] = (
            dot_over(grad_pre, w_in[...], 1, 1).astype(jnp.bfloat16).reshape(4, cap, depth)
        )
        core_sum(k).start()
        grad_out[...] += dot_over(hidden, grads, 0, 0)
        grad_in[...] += dot_over(normed, grad_pre, 0, 0)

    def stage_core(k):
        f = block(k)
        core_sum(k).wait_recv()
        x_send[f] = (
            part[f, own_x].astype(jnp.float32) + core_got[f, 1 - x].astype(jnp.float32)
        ).astype(jnp.bfloat16)
        x_sum(k).start()
        kept[f] = part[f, own].astype(jnp.float32) + core_got[f, x].astype(jnp.float32)

    def stage_back(k):
        f = block(k)
        x_sum(k).wait_recv()
        total = (kept[f] + x_got[f].astype(jnp.float32)).astype(jnp.bfloat16)

        @pl.when(k == 0)
        def _():
            back[e] = total

        @pl.when(k > 0)
        def _():
            final[f] = total
            give_back(k, e).start()

    stages = (
        (1, stage_forward),
        (3, stage_back),
        (2, stage_core),
        (1, stage_compute),
        (0, stage_spread),
    )

    def step(t, carry):
        for lag, stage in stages:
            k = t - lag

            @pl.when((k >= 0) & (k < count))
            def _(stage=stage, k=k):
                stage(k)

        return carry

    lax.fori_loop(0, count + 3, step, 0)

    def finish(k, carry):
        @pl.when(k > 0)
        def _():
            dispatch(k).wait_send()
            give_back(k, e).wait_send()
            give_back(k, (e + k) % count).wait_recv()

        near(1, k, own, x_peer).wait_send()
        near(2, k, own, core_peer).wait_send()
        near(3, k, own_x, core_peer).wait_send()
        core_sum(k).wait_send()
        x_sum(k).wait_send()
        return carry

    lax.fori_loop(0, count, finish, 0)


def moe(packed, w_in, w_out):
    count, cap, width = packed.shape
    vmem = pl.BlockSpec(memory_space=pltpu.VMEM)
    half = jnp.bfloat16
    return pl.pallas_call(
        moe_kernel,
        out_shape=(
            jax.ShapeDtypeStruct(packed.shape, half),
            jax.ShapeDtypeStruct(w_in.shape, jnp.float32),
            jax.ShapeDtypeStruct(w_out.shape, jnp.float32),
        ),
        in_specs=[vmem] * 3,
        out_specs=(vmem,) * 3,
        scratch_shapes=[
            pltpu.VMEM((count, 4, cap, width), half),
            pltpu.VMEM((count, 4, cap, width), half),
            pltpu.VMEM((count, 2, cap, width), half),
            pltpu.VMEM((count, cap, width), half),
            pltpu.VMEM((count, cap, width), half),
            pltpu.VMEM((count, cap, width), jnp.float32),
            pltpu.VMEM((count, cap, width), half),
            pltpu.SemaphoreType.DMA((2, 7, count)),
        ],
        compiler_params=pltpu.CompilerParams(
            collective_id=0, has_side_effects=True, vmem_limit_bytes=56 * 2**20
        ),
    )(packed, w_in, w_out)


def sum_kernel(terms, totals, near_got, near_sum, far_got, sems):
    seq_size = lax.axis_size("seq")
    seq, dp = lax.axis_index("seq"), lax.axis_index("dp")
    groups = terms.shape[1]
    m, h = seq % 4, dp * (seq_size // 4) + seq // 4

    def mate(j):
        return {"dp": dp, "seq": seq // 4 * 4 + (m + j) % 4}

    def peer(j):
        number = (h + j) % groups * 4 + m
        return {"dp": number // seq_size, "seq": number % seq_size}

    def copy(phase, j, source, target, device):
        return pltpu.make_async_remote_copy(
            src_ref=source,
            dst_ref=target,
            send_sem=sems.at[phase, 0, j],
            recv_sem=sems.at[phase, 1, j],
            device_id=device,
            device_id_type=MESH,
        )

    def every(size, action):
        def one(j, carry):
            action(j)
            return carry

        lax.fori_loop(1, size, one, 0)

    def behind_m(j):
        return (m + 4 - j) % 4

    def behind_h(j):
        return (h + groups - j) % groups

    def near_in(j, slot):
        return copy(0, j, terms.at[(m + j) % 4], near_got.at[slot], mate(j))

    def far_in(j, slot):
        return copy(1, j, near_sum.at[(h + j) % groups], far_got.at[slot], peer(j))

    def far_out(j, slot):
        return copy(2, j, totals.at[m, h], totals.at[m, slot], peer(j))

    def near_out(j, slot):
        return copy(3, j, totals.at[m], totals.at[slot], mate(j))

    barrier = pltpu.get_barrier_semaphore()

    def greet(device):
        pl.semaphore_signal(barrier, inc=1, device_id=device, device_id_type=MESH)

    every(4, lambda j: greet(mate(j)))
    every(groups, lambda j: greet(peer(j)))
    pl.semaphore_wait(barrier, groups + 2)
    every(4, lambda j: near_in(j, m).start())
    near_got[m] = terms[m]
    every(4, lambda j: near_in(j, behind_m(j)).wait_recv())
    near_sum[...] = jnp.sum(near_got[...], axis=0)
    every(groups, lambda j: far_in(j, h).start())
    far_got[h] = near_sum[h]
    every(groups, lambda j: far_in(j, behind_h(j)).wait_recv())
    totals[m, h] = jnp.sum(far_got[...], axis=0)
    every(groups, lambda j: far_out(j, h).start())
    every(groups, lambda j: far_out(j, behind_h(j)).wait_recv())
    every(4, lambda j: near_out(j, m).start())
    every(4, lambda j: near_out(j, behind_m(j)).wait_recv())
    every(4, lambda j: near_in(j, m).wait_send())
    every(groups, lambda j: far_in(j, h).wait_send())
    every(groups, lambda j: far_out(j, h).wait_send())
    every(4, lambda j: near_out(j, m).wait_send())


def sum_everywhere(rows):
    groups = lax.axis_size("seq") * lax.axis_size("dp") // 4
    size = rows.size
    tall = -(-size // (groups * 4 * 1024)) * 8
    padded = jnp.pad(rows.reshape(-1), (0, groups * 4 * tall * 128 - size)).reshape(
        4, groups, tall, 128
    )
    vmem = pl.BlockSpec(memory_space=pltpu.VMEM)
    totals = pl.pallas_call(
        sum_kernel,
        out_shape=jax.ShapeDtypeStruct(padded.shape, jnp.float32),
        in_specs=[vmem],
        out_specs=vmem,
        scratch_shapes=[
            pltpu.VMEM(padded.shape, jnp.float32),
            pltpu.VMEM(padded.shape[1:], jnp.float32),
            pltpu.VMEM(padded.shape[1:], jnp.float32),
            pltpu.SemaphoreType.DMA((4, 2, max(groups, 4))),
        ],
        compiler_params=pltpu.CompilerParams(collective_id=1, has_side_effects=True),
    )(padded)
    return totals.reshape(-1)[:size].reshape(rows.shape)


def body(frames, kernel, norm_gain, router, experts, w_in, w_out, cotangent):
    inputs_dev = frames[0]
    row_count = inputs_dev.shape[0]
    width = inputs_dev.shape[1]
    length = kernel.shape[0]
    half_width = length // 2
    expert_count = router.shape[1]
    top_count = experts.shape[2]
    capacity = 2 * row_count * top_count // expert_count
    in_weights = w_in[0]
    out_weights = w_out[0]
    padded = padded_2(inputs_dev, (("seq", 0),), half_width)
    summed, normed_b = conv_norm(padded, kernel, norm_gain, row_count)
    choice_ids = experts[0]
    gate_one, gate_two, pick_diff = gate_values(
        normed_b, router, choice_ids[:, 0], choice_ids[:, 1]
    )
    flat_ids = choice_ids.reshape(-1)
    slot_index = slot_numbers(flat_ids, expert_count)
    position = flat_ids * capacity + slot_index
    dispatch_table = (
        lax.broadcasted_iota(jnp.int32, (expert_count * capacity, flat_ids.shape[0]), 0)
        == position[None, :]
    ).astype(jnp.bfloat16)

    def pack(values):
        return jnp.dot(dispatch_table, values, preferred_element_type=jnp.float32).astype(
            jnp.bfloat16
        )

    repeated = jnp.repeat(normed_b, top_count, axis=0)
    upstream = cotangent[0].astype(jnp.float32)
    grad_assigned = jnp.stack([gate_one[:, None] * upstream, gate_two[:, None] * upstream], axis=1)
    grad_values = grad_assigned.reshape(row_count * top_count, width).astype(jnp.bfloat16)
    packed = pack(jnp.concatenate([repeated, grad_values], axis=1))
    back, in_term, out_term = moe(
        packed.reshape(expert_count, capacity, 2 * width), in_weights, out_weights
    )
    back = back.reshape(expert_count * capacity, 2 * width)
    assigned = dot_over(dispatch_table, back[:, :width], 0, 0).reshape(
        row_count, top_count, width
    )
    out_one = assigned[:, 0]
    out_two = assigned[:, 1]
    mixed = (summed + gate_one[:, None] * out_one + gate_two[:, None] * out_two).astype(
        jnp.bfloat16
    )
    both = jnp.sum(dispatch_table.reshape(-1, row_count, top_count), axis=2)
    normed_grads = dot_over(both, back[:, width:], 0, 0)
    router_term, normed_term = gate_backward(
        upstream, out_one, out_two, gate_one, gate_two, pick_diff, normed_b, router
    )
    pullback = jax.vjp(normalize, summed, norm_gain)[1]
    summed_grad, gain_term = pullback(normed_grads + normed_term)
    upstream_total = upstream + summed_grad
    padded_grad = padded_2(upstream_total.astype(jnp.bfloat16), (("seq", 0),), half_width).astype(
        upstream_total.dtype
    )
    grad_frames = (upstream_total + conv_transpose(padded_grad, kernel, row_count)).astype(
        jnp.bfloat16
    )
    kernel_term = kernel_terms(padded, upstream_total, length, row_count)
    sums = sum_everywhere(
        jnp.concatenate([kernel_term, gain_term[None], router_term.T], axis=0)
    )
    grad_kernel, grad_gain = sums[:length], sums[length]
    grad_router = sums[length + 1 :].T
    grad_in, grad_out = in_term, out_term
    if lax.axis_size("dp") > 1:
        grad_in, grad_out = (
            lax.psum(in_term.astype(jnp.bfloat16), "dp").astype(jnp.float32),
            lax.psum(out_term.astype(jnp.bfloat16), "dp").astype(jnp.float32),
        )
    return (
        mixed[None],
        grad_frames[None],
        grad_kernel,
        grad_gain,
        grad_router,
        grad_in[None],
        grad_out[None],
    )


def solution(mesh):
    return jax.shard_map(
        body,
        mesh=mesh,
        in_specs=(
            P("dp", "seq", None),
            P(),
            P(),
            P(),
            P("dp", "seq", None),
            P("seq", None, None),
            P("seq", None, None),
            P("dp", "seq", None),
        ),
        out_specs=(
            P("dp", "seq", None),
            P("dp", "seq", None),
            P(),
            P(),
            P(),
            P("seq", None, None),
            P("seq", None, None),
        ),
        check_vma=False,
    )
```
